512 devices in a mesh: pool: 16 (over x, y), dcp: 32 (over z, core).
Axes of the slice: x: 4, y: 4, z: 16, core: 2. Of those that a mesh axis runs over, the one named last changes fastest.
Arguments:
- q_latent: bfloat16 [16, 4, 64, 512], P('pool'), may hold values from -70 to 70
- q_rope: bfloat16 [16, 4, 4096], P('pool'), may hold values from -6 to 6
- pool_latent: bfloat16 [24576, 64, 512], P(('pool', 'dcp')), may hold values from -6 to 6
- pool_rope: bfloat16 [24576, 4096], P(('pool', 'dcp')), may hold values from -6 to 6
- page_table: int32 [16, 1536], replicated, may hold values from -1 to 24575, as said below
- lengths: int32 [16], replicated, may hold values from 1 to 98304, as said below
- slot_request: int32 [16], replicated, may hold values from 0 to 15, each once
Outputs:
- context: bfloat16 [16, 4, 64, 512], P('pool', None, 'dcp')
- log_total: float32 [16, 4, 64], P('pool', None, 'dcp')
The draws below stay inside these ranges and needn't reach their ends.
Inputs may be any that keep to these rules, and one draw needn't show every extreme that they name: `page_table`: entry k of row r is -1 exactly when k * 64 >= lengths[r], else a row of pool_latent; no row is named twice. Row index // 48 is the device that holds it (pool index times the size of dcp plus dcp index). Each device holds at most 3 pages of one request, and exactly 3 pages of the longest request. `lengths`: one request has 98304 tokens.
All inputs are finite; a program needn't handle non-finite values.
Results may differ from the reference program's by a relative error of at most 0.003.
Values may be sent and summed in bfloat16 or wider, within the bound.
A program may use at most 64 MiB of HBM per device.

```python
import jax
import jax.numpy as jnp
from jax import lax

H = 64
C = 512
R = 64
QK_NOPE = 128
QUERIES = 4
PAGE = 64
CAP = 3
REQUESTS = 16
POOL_SLOTS = 48
MAXP = 1536
N_DCP = 32
DEVICES = 512


def page_counts(key):
    key = jax.random.fold_in(key, 11)
    first, second, third = jax.random.split(key, 3)
    left = jax.random.randint(first, (REQUESTS,), 0, MAXP)
    right = jax.random.randint(second, (REQUESTS,), 0, MAXP)
    counts = jnp.maximum(1, left * right // MAXP)
    longest = jax.random.randint(third, (), 0, REQUESTS)
    return jnp.where(jnp.arange(REQUESTS) == longest, MAXP, counts).astype(jnp.int32)


def draw_lengths(key, part):
    counts = page_counts(key)
    key = jax.random.fold_in(key, 1)
    tail = jax.random.randint(key, (REQUESTS,), 1, PAGE + 1)
    tail = jnp.where(counts == MAXP, PAGE, tail)
    return ((counts - 1) * PAGE + tail).astype(jnp.int32)


def draw_page_table(key, part):
    counts = page_counts(key)
    key = jax.random.fold_in(key, 2)
    first, second = jax.random.split(key)
    owners = MAXP // CAP
    cells = jnp.broadcast_to(jnp.arange(MAXP, dtype=jnp.int32), (REQUESTS, MAXP))
    cells = jax.random.permutation(first, cells, axis=1, independent=True)
    holder = cells // CAP
    within = cells % CAP
    slots = jnp.broadcast_to(jnp.arange(POOL_SLOTS, dtype=jnp.int32), (owners, POOL_SLOTS))
    slots = jax.random.permutation(second, slots, axis=1, independent=True)
    request = jnp.arange(REQUESTS, dtype=jnp.int32)[:, None]
    local_rows = slots.reshape(-1)[holder * POOL_SLOTS + request * CAP + within]
    table = holder * POOL_SLOTS + local_rows
    used = jnp.arange(MAXP, dtype=jnp.int32)[None, :] < counts[:, None]
    return jnp.where(used, table, -1).astype(jnp.int32)


def draw_q_latent(key, part):
    key = jax.random.fold_in(key, 3)
    shape = (REQUESTS, QUERIES, H, C)
    values = 1.7 * jnp.clip(jax.random.normal(key, shape, jnp.float32), -6.0, 6.0)
    return values.astype(jnp.bfloat16)


def levels(stream_key, dims, pieces, least, high):
    loudness = 1.0
    for axis_at, blocks in pieces:
        draws = jax.random.uniform(jax.random.fold_in(jax.random.fold_in(stream_key, 6), axis_at), (blocks,), jnp.float32, least / len(pieces), high / len(pieces))
        loudness = loudness * jnp.repeat(jnp.exp(draws), dims[axis_at] // blocks).reshape((-1,) + (1,) * (len(dims) - 1 - axis_at))
    return loudness


def centred(rng, dims, spread, reach, shards=(), kind=jnp.bfloat16):
    entries = spread * jax.random.normal(rng, dims, jnp.float32)
    if shards:
        entries = entries * levels(rng, dims, shards, -0.22, 0.18)
    return jnp.clip(entries, -reach, reach).astype(kind)


def setup_inputs(seed: int = 0) -> dict:
    arg_keys = jax.random.split(jax.random.key(seed), 8)
    return {
        "q_latent": draw_q_latent(jax.random.fold_in(arg_keys[7], 71), 0),
        "q_rope": centred(arg_keys[1], (REQUESTS, QUERIES, H * R), 1.7, 6.0, ((0, 16),)),
        "pool_latent": centred(arg_keys[2], (DEVICES * POOL_SLOTS, PAGE, C), 1.0, 6.0, ((0, 512),)),
        "pool_rope": centred(arg_keys[3], (DEVICES * POOL_SLOTS, PAGE * R), 1.0, 6.0, ((0, 512),)),
        "page_table": draw_page_table(jax.random.fold_in(arg_keys[7], 71), 0),
        "lengths": draw_lengths(jax.random.fold_in(arg_keys[7], 71), 0),
        "slot_request": jax.random.permutation(arg_keys[6], REQUESTS).astype(jnp.int32),
    }


NEGATIVE = -1.0e30


def reference(q_latent, q_rope, pool_latent, pool_rope, page_table, lengths, slot_request):
    factor = (QK_NOPE + R) ** -0.5
    contract = (((1,), (1,)), ((), ()))
    span = MAXP * PAGE
    per_class = span // N_DCP

    def attend(slot_index):
        request = slot_request[slot_index]
        row_list = page_table[request]
        present = row_list >= 0
        rows_safe = jnp.where(present, row_list, 0).astype(jnp.int32)
        cached = pool_latent[rows_safe].reshape(span, C)
        key_rope = pool_rope[rows_safe].reshape(span, R)
        position = jnp.arange(span, dtype=jnp.int32)
        usable = jnp.repeat(present, PAGE, total_repeat_length=span) & (position < lengths[request])
        queries = q_latent[slot_index].reshape(QUERIES * H, C)
        query_rope = q_rope[slot_index].reshape(QUERIES * H, R)
        scores = lax.dot_general(queries, cached, contract, preferred_element_type=jnp.float32)
        scores = (scores + lax.dot_general(query_rope, key_rope, contract, preferred_element_type=jnp.float32)) * factor
        scores = jnp.where(usable[None, :], scores, NEGATIVE)
        grouped = scores.reshape(QUERIES * H, per_class, N_DCP)
        usable_grouped = usable.reshape(per_class, N_DCP)
        part_top = jnp.max(grouped, axis=1)
        weights = jnp.where(usable_grouped[None], jnp.exp(grouped - part_top[:, None, :]), 0.0).astype(jnp.bfloat16)
        part_total = jnp.sum(weights.astype(jnp.float32), axis=1)
        weights_class = weights.astype(jnp.float32).transpose(2, 0, 1)
        cached_class = cached.astype(jnp.float32).reshape(per_class, N_DCP, C).transpose(1, 0, 2)
        part_blend = lax.dot_general(weights_class, cached_class, (((2,), (1,)), ((0,), (0,))), precision=lax.Precision.HIGHEST, preferred_element_type=jnp.float32)
        top_score = jnp.max(part_top, axis=1)
        rescale = jnp.exp(part_top - top_score[:, None])
        totals = jnp.sum(rescale * part_total, axis=1)
        blended = jnp.sum(rescale.T[:, :, None] * part_blend, axis=0)
        context = (blended / totals[:, None]).astype(jnp.bfloat16).reshape(QUERIES, H, C)
        log_total = (top_score + jnp.log(totals)).reshape(QUERIES, H)
        return context, log_total

    context, log_total = lax.map(attend, jnp.arange(REQUESTS, dtype=jnp.int32))
    return context, log_total
```

```python
import functools

import jax
import jax.numpy as jnp
from jax import lax
from jax.experimental import pallas as pl
from jax.experimental.pallas import tpu as pltpu
from jax.sharding import PartitionSpec as P

MESH = pl.DeviceIdType.MESH
QK_NOPE = 128
NEG = -1e30
EMPTY = -1e29

SIDE = 4
RING = 16
PAGES = 48
CAP = 3
TOK = 64
LAT = 512
ROPE = 64
ROWS = 256
HALF = 128
SPAN = 768
MAXP = 1536

SENDS = (
    (1, 2, 1), (1, 1, 2), (1, 3, 2), (0, 2, 2), (0, 1, 1), (0, 3, 1),
    (1, 2, 0), (1, 1, 3), (1, 3, 3), (0, 2, 3), (0, 1, 0), (0, 3, 0),
)
ORDER = (1, 2, 3, 0)


def dot(a, b):
    return jnp.dot(a, b, preferred_element_type=jnp.float32)


def dot_t(a, b):
    return lax.dot_general(a, b, (((1,), (1,)), ((), ())), preferred_element_type=jnp.float32)


def iota(shape, dim):
    return lax.broadcasted_iota(jnp.int32, shape, dim)


def kernel(
    slot_s, len_s, table, ql, qr, lat_hbm, rope_hbm,
    ctx_out, log_out,
    lat_v, rope_v, rope_f, tab_p, tab_r, idx_v, idx_s,
    stage_l, stage_r, kv, kr, krx, qs, qcat, s_ref, p_ref,
    acc, st, r0_acc, r0_st, h_acc, h_st, r1_acc, r1_st, fin, zbuf,
    load_sem, idx_sem, kv_send, kv_recv, kr_send, kr_recv,
    q_send, q_recv, f_send, f_recv, r0_send, r0_recv, r1_send, r1_recv, z_send, z_recv,
):
    pool = lax.axis_index("pool")
    member = lax.axis_index("dcp")
    px, py = pool // SIDE, pool % SIDE
    z, core = member // 2, member % 2

    def wrap(v):
        return lax.rem(v + 2 * SIDE, SIDE)

    def axes(x, y):
        odd = lax.rem(x + y, 2)
        return ((odd, 1 - odd), (1 - odd, odd))

    def shift(x, y, unit, steps):
        return wrap(x + steps * unit[0]), wrap(y + steps * unit[1])

    def group_at(x, y, place):
        other, key = axes(x, y)
        if place == 0:
            gx, gy = x, y
        elif place == 1:
            gx, gy = shift(x, y, other, 2)
        elif place == 2:
            gx, gy = shift(x, y, key, 1)
        else:
            gx, gy = shift(x, y, key, 3)
        return gx * SIDE + gy

    mine = axes(px, py)

    def peer(axis, steps):
        x, y = shift(px, py, mine[axis], steps)
        return (x * SIDE + y, member)

    sibling = (pool, z * 2 + 1 - core)

    def around(steps):
        return (pool, lax.rem(z + steps, RING) * 2 + core)

    load_l = pltpu.make_async_copy(lat_hbm, lat_v, load_sem.at[0])
    load_r = pltpu.make_async_copy(rope_hbm, rope_v, load_sem.at[1])
    load_r.start()
    load_l.start()

    barrier = pltpu.get_barrier_semaphore()
    greet = [peer(axis, steps) for axis in (0, 1) for steps in (1, 2, 3)]
    greet += [sibling] + [around(steps) for steps in range(1, RING)]
    for device in greet:
        pl.semaphore_signal(barrier, inc=1, device_id=device, device_id_type=MESH)

    device = pool * 32 + member
    for g in range(16):
        tab_p[pl.ds(g, 1), :] = table[pl.ds(slot_s[g], 1), :] - device * PAGES
    groups = [group_at(px, py, a) for a in range(4)]
    for a in range(4):
        row = table[pl.ds(slot_s[groups[a]], 1), :]
        for b in range(4):
            x, y = shift(px, py, mine[1] if a < 2 else mine[0], b)
            tab_r[pl.ds(4 * a + b, 1), :] = row - ((x * SIDE + y) * 32 + member) * PAGES

    def picks(tab):
        local = jnp.where((tab >= 0) & (tab < PAGES), tab, 64)
        found = []
        for _ in range(CAP):
            first = jnp.min(local, axis=1, keepdims=True)
            found.append(first)
            local = jnp.where(local > first, local, 64)
        return found

    def lanes(values):
        lane = iota((16, 128), 1)
        out = jnp.zeros((16, 128), jnp.int32)
        for j in range(CAP):
            out = jnp.where(lane == j, values[j], out)
        return out

    idx_v[0:16, :] = lanes([jnp.minimum(v, PAGES - 1) for v in picks(tab_p[...])])
    tab = tab_r[...]
    page = iota((16, MAXP), 1)
    quarter = iota((16, 1), 0) // 4
    length = jnp.zeros((16, 1), jnp.int32)
    for a in range(4):
        length = jnp.where(quarter == a, len_s[slot_s[groups[a]]], length)
    counts = []
    for first in picks(tab):
        number = jnp.sum(jnp.where(tab == first, page, 0), axis=1, keepdims=True)
        count = jnp.clip(length - number * TOK, 0, TOK)
        counts.append(jnp.where(first < 64, count, 0))
    idx_v[16:32, :] = lanes(counts)
    to_smem = pltpu.make_async_copy(idx_v, idx_s, idx_sem)
    to_smem.start()

    def parts(shape):
        r = iota(shape, 0)
        return r // HALF, (r // 8) % RING, (r // 2) % 4, r % 2

    c_, z_, q_, h_ = parts((ROWS, ROWS))
    perm = (iota((ROWS, ROWS), 1) == q_ * 64 + 4 * z_ + 2 * c_ + h_).astype(jnp.bfloat16)
    qcat[0, :, 0:LAT] = dot(perm, ql[...]).astype(jnp.bfloat16)
    rope_rows = qr[...].astype(jnp.float32)
    for i in range(32):
        qs[4 * i : 4 * i + 4, :] = rope_rows[:, 128 * i : 128 * i + 128]
    c_, z_, q_, h_ = parts((ROWS, 128))
    pick = (iota((ROWS, 128), 1) == (2 * z_ + c_) * 4 + q_).astype(jnp.bfloat16)
    pair = dot(pick, qs[...].astype(jnp.bfloat16))
    swapped = jnp.concatenate([pair[:, 64:128], pair[:, 0:64]], axis=1)
    qcat[0, :, LAT : LAT + 128] = jnp.where(
        iota((ROWS, 128), 1) // 64 == h_, pair, swapped
    ).astype(jnp.bfloat16)

    load_r.wait()
    for i in range(32):
        rope_f[PAGES * i : PAGES * i + PAGES, :] = rope_v[:, 128 * i : 128 * i + 128].astype(
            jnp.float32
        )
    to_smem.wait()
    load_l.wait()

    def take(group, j):
        slot = idx_s[group, j]
        return lat_v[slot], rope_f[pl.ds(slot, 32, stride=PAGES), :].astype(jnp.bfloat16)

    pl.semaphore_wait(barrier, len(greet))

    half = pl.ds(pl.multiple_of(core * HALF, HALF), HALF)
    rest = pl.ds(pl.multiple_of((1 - core) * HALF, HALF), HALF)
    query = {}
    for steps, place in ((1, 3), (3, 2), (2, 1)):
        query[place] = pltpu.make_async_remote_copy(
            src_ref=qcat.at[0, half],
            dst_ref=qcat.at[place, half],
            send_sem=q_send.at[place],
            recv_sem=q_recv.at[place],
            device_id=peer(0, steps),
            device_id_type=MESH,
        )
        query[place].start()

    sent = {}
    for i, (axis, steps, place) in enumerate(SENDS):
        tx, ty = shift(px, py, mine[axis], steps)
        group = group_at(tx, ty, place)
        for j in range(CAP):
            latent, rope = take(group, j)
            stage_l[i, j] = latent
            stage_r[i, j] = rope
        source = 4 - steps
        pair_of = (
            pltpu.make_async_remote_copy(
                src_ref=stage_l.at[i],
                dst_ref=kv.at[place, :, source],
                send_sem=kv_send.at[i],
                recv_sem=kv_recv.at[place, source],
                device_id=(tx * SIDE + ty, member),
                device_id_type=MESH,
            ),
            pltpu.make_async_remote_copy(
                src_ref=stage_r.at[i],
                dst_ref=kr.at[place, :, source],
                send_sem=kr_send.at[i],
                recv_sem=kr_recv.at[place, source],
                device_id=(tx * SIDE + ty, member),
                device_id_type=MESH,
            ),
        )
        for copy in pair_of:
            copy.start()
        sent[place, source] = pair_of

    for a in range(4):
        for j in range(CAP):
            latent, rope = take(groups[a], j)
            kv[a, j, 0] = latent
            kr[a, j, 0] = rope

    passed = {}
    for place in (2, 3, 1):
        query[place].wait_recv()
        passed[place] = pltpu.make_async_remote_copy(
            src_ref=qcat.at[place, half],
            dst_ref=qcat.at[place, half],
            send_sem=f_send.at[place],
            recv_sem=f_recv.at[place],
            device_id=sibling,
            device_id_type=MESH,
        )
        passed[place].start()

    factor = (QK_NOPE + ROPE) ** (-0.5)
    expand = (iota((256, 128), 0) // 2 == iota((256, 128), 1)).astype(jnp.bfloat16)
    parity = iota((256, 128), 1) // 64 == iota((256, 128), 0) % 2
    within = iota((1, 256), 1) % TOK
    source_of = iota((1, 256), 1) // TOK
    lane = iota((HALF, 128), 1)

    def attend(a):
        for j in range(CAP):
            pairs = kr[a, j].reshape(128, 128)
            krx[...] = jnp.where(parity, dot(expand, pairs), 0.0).astype(jnp.bfloat16)
            keys = kv[a, j].reshape(256, LAT)
            scores = dot_t(qcat[a, :, 0:LAT], keys) + dot_t(qcat[a, :, LAT:], krx[...])
            limit = jnp.zeros((1, 256), jnp.int32)
            for b in range(4):
                limit = jnp.where(source_of == b, idx_s[16 + 4 * a + b, j], limit)
            s_ref[:, 256 * j : 256 * j + 256] = jnp.where(within < limit, scores * factor, NEG)
        for block in range(4):
            rows = slice(64 * block, 64 * block + 64)
            s = s_ref[rows, :]
            top = jnp.maximum(jnp.max(s, axis=1, keepdims=True), EMPTY)
            p = jnp.exp(s - top).astype(jnp.bfloat16)
            p_ref[rows, :] = p
            total = jnp.sum(p.astype(jnp.float32), axis=1, keepdims=True)
            l64 = iota((64, 128), 1)
            st[a, rows, :] = jnp.where(l64 == 0, top, jnp.where(l64 == 1, total, 0.0))
        acc[a] = dot(p_ref[...], kv[a].reshape(SPAN, LAT))

    def merge(parts_):
        top = functools.reduce(jnp.maximum, [t for _, t, _ in parts_])
        scales = [jnp.exp(t - top) for _, t, _ in parts_]
        total = sum(w * l for w, (_, _, l) in zip(scales, parts_))
        sums = sum(w * v for w, (v, _, _) in zip(scales, parts_))
        return sums, top, total

    exchange, returned = {}, {}

    def swap(a):
        exchange[a] = (
            pltpu.make_async_remote_copy(
                src_ref=acc.at[a, rest],
                dst_ref=r0_acc.at[a],
                send_sem=r0_send.at[a, 0],
                recv_sem=r0_recv.at[a, 0],
                device_id=sibling,
                device_id_type=MESH,
            ),
            pltpu.make_async_remote_copy(
                src_ref=st.at[a, rest],
                dst_ref=r0_st.at[a],
                send_sem=r0_send.at[a, 1],
                recv_sem=r0_recv.at[a, 1],
                device_id=sibling,
                device_id_type=MESH,
            ),
        )
        for copy in exchange[a]:
            copy.start()

    def halves(a):
        for copy in exchange[a]:
            copy.wait_recv()
        own = st[a, half, :]
        other = r0_st[a]
        return [
            (acc[a, half, :], own[:, 0:1], own[:, 1:2]),
            (r0_acc[a], other[:, 0:1], other[:, 1:2]),
        ]

    def give_back(a):
        sums, top, total = merge(halves(a))
        h_acc[a - 1] = sums
        stats = jnp.where(lane == 0, top, jnp.where(lane == 1, total, 0.0))
        h_st[a - 1] = stats.T[0:8, :]
        axis, steps = {1: (0, 2), 2: (1, 1), 3: (1, 3)}[a]
        slot = {1: 1, 2: 2, 3: 0}[a]
        returned[a] = (
            pltpu.make_async_remote_copy(
                src_ref=h_acc.at[a - 1],
                dst_ref=r1_acc.at[slot],
                send_sem=r1_send.at[slot, 0],
                recv_sem=r1_recv.at[slot, 0],
                device_id=peer(axis, steps),
                device_id_type=MESH,
            ),
            pltpu.make_async_remote_copy(
                src_ref=h_st.at[a - 1],
                dst_ref=r1_st.at[slot],
                send_sem=r1_send.at[slot, 1],
                recv_sem=r1_recv.at[slot, 1],
                device_id=peer(axis, steps),
                device_id_type=MESH,
            ),
        )
        for copy in returned[a]:
            copy.start()

    pending = None
    for a in ORDER:
        if a:
            passed[a].wait_recv()
        for source in (1, 2, 3):
            for copy in sent[a, source]:
                copy.wait_recv()
        attend(a)
        swap(a)
        if pending is not None:
            give_back(pending)
        pending = a

    pieces = halves(0)
    for a in (1, 2, 3):
        for copy in returned[a]:
            copy.wait_recv()
    for slot in range(3):
        back = jnp.concatenate([r1_st[slot], jnp.zeros((120, 128), jnp.float32)], axis=0).T
        pieces.append((r1_acc[slot], back[:, 0:1], back[:, 1:2]))
    sums, top, total = merge(pieces)
    fin[:, 0:LAT] = sums
    fin[:, LAT:] = jnp.where(lane == 0, top, jnp.where(lane == 1, total, 0.0))

    spread = []
    for steps in range(1, RING):
        rows = pl.ds(pl.multiple_of(lax.rem(z + steps, RING) * 8, 8), 8)
        copy = pltpu.make_async_remote_copy(
            src_ref=fin.at[rows],
            dst_ref=zbuf.at[steps],
            send_sem=z_send.at[steps],
            recv_sem=z_recv.at[steps],
            device_id=around(steps),
            device_id_type=MESH,
        )
        copy.start()
        spread.append(copy)
    zbuf[0] = fin[pl.ds(pl.multiple_of(z * 8, 8), 8), :]
    for copy in spread:
        copy.wait_recv()
    pieces = [
        (zbuf[i, :, 0:LAT], zbuf[i, :, LAT : LAT + 1], zbuf[i, :, LAT + 1 : LAT + 2])
        for i in range(RING)
    ]
    sums, top, total = merge(pieces)
    ctx_out[...] = sums / total
    log_out[...] = jnp.broadcast_to(top + jnp.log(total), (8, 128))

    for copy in spread:
        copy.wait_send()
    for place in (1, 2, 3):
        query[place].wait_send()
        passed[place].wait_send()
        for copy in returned[place]:
            copy.wait_send()
    for a in range(4):
        for copy in exchange[a]:
            copy.wait_send()
    for pair_of in sent.values():
        for copy in pair_of:
            copy.wait_send()


def per_device(q_latent, q_rope, pool_latent, pool_rope, page_table, lengths, slot_request):
    vmem = pl.BlockSpec(memory_space=pltpu.VMEM)
    smem = pl.BlockSpec(memory_space=pltpu.SMEM)
    anywhere = pl.BlockSpec(memory_space=pl.ANY)
    f32, bf16, i32 = jnp.float32, jnp.bfloat16, jnp.int32
    dma = pltpu.SemaphoreType.DMA
    ctx, log = pl.pallas_call(
        kernel,
        out_shape=(jax.ShapeDtypeStruct((8, LAT), f32), jax.ShapeDtypeStruct((8, 128), f32)),
        in_specs=[smem, smem, vmem, vmem, vmem, anywhere, anywhere],
        out_specs=(vmem, vmem),
        scratch_shapes=[
            pltpu.VMEM((PAGES, TOK, LAT), bf16),
            pltpu.VMEM((PAGES, TOK * ROPE), bf16),
            pltpu.VMEM((32 * PAGES, 128), f32),
            pltpu.VMEM((16, MAXP), i32),
            pltpu.VMEM((16, MAXP), i32),
            pltpu.VMEM((32, 128), i32),
            pltpu.SMEM((32, 128), i32),
            pltpu.VMEM((12, CAP, TOK, LAT), bf16),
            pltpu.VMEM((12, CAP, 32, 128), bf16),
            pltpu.VMEM((4, CAP, 4, TOK, LAT), bf16),
            pltpu.VMEM((4, CAP, 4, 32, 128), bf16),
            pltpu.VMEM((256, 128), bf16),
            pltpu.VMEM((128, 128), f32),
            pltpu.VMEM((4, ROWS, LAT + 128), bf16),
            pltpu.VMEM((ROWS, SPAN), f32),
            pltpu.VMEM((ROWS, SPAN), bf16),
            pltpu.VMEM((4, ROWS, LAT), f32),
            pltpu.VMEM((4, ROWS, 128), f32),
            pltpu.VMEM((4, HALF, LAT), f32),
            pltpu.VMEM((4, HALF, 128), f32),
            pltpu.VMEM((3, HALF, LAT), f32),
            pltpu.VMEM((3, 8, 128), f32),
            pltpu.VMEM((3, HALF, LAT), f32),
            pltpu.VMEM((3, 8, 128), f32),
            pltpu.VMEM((HALF, LAT + 128), f32),
            pltpu.VMEM((RING, 8, LAT + 128), f32),
            dma((2,)),
            dma,
            dma((12,)),
            dma((4, 4)),
            dma((12,)),
            dma((4, 4)),
            dma((4,)),
            dma((4,)),
            dma((4,)),
            dma((4,)),
            dma((4, 2)),
            dma((4, 2)),
            dma((3, 2)),
            dma((3, 2)),
            dma((RING,)),
            dma((RING,)),
        ],
        compiler_params=pltpu.CompilerParams(
            collective_id=0, has_side_effects=True, vmem_limit_bytes=48 * 2**20
        ),
        cost_estimate=pl.CostEstimate(flops=2 * 10**9, bytes_accessed=4 * 10**6, transcendentals=10**6),
    )(
        slot_request,
        lengths,
        page_table,
        q_latent.reshape(ROWS, LAT),
        q_rope.reshape(4, 64 * ROPE),
        pool_latent,
        pool_rope,
    )
    context = ctx.astype(bf16).reshape(1, 4, 2, LAT)
    return context, log[:, 0].reshape(1, 4, 2)


def solution(mesh):
    in_specs = (
        P("pool", None, None, None),
        P("pool", None, None),
        P(("pool", "dcp"), None, None),
        P(("pool", "dcp"), None),
        P(),
        P(),
        P(),
    )
    out_specs = (P("pool", None, "dcp", None), P("pool", None, "dcp"))
    return jax.shard_map(
        per_device, mesh=mesh, in_specs=in_specs, out_specs=out_specs, check_vma=False
    )
```

```python
import functools

import jax
import jax.numpy as jnp
from jax import lax
from jax.experimental import pallas as pl
from jax.experimental.pallas import tpu as pltpu
from jax.sharding import PartitionSpec as P

MESH = pl.DeviceIdType.MESH
QK_NOPE = 128
NEG = -1e30
EMPTY = -1e29

SIDE = 4
RING = 16
PAGES = 48
CAP = 3
TOK = 64
LAT = 512
ROPE = 64
ROWS = 256
HALF = 128
SPAN = 768
MAXP = 1536

SENDS = (
    (1, 2, 1), (1, 1, 2), (1, 3, 2), (0, 2, 2), (0, 1, 1), (0, 3, 1),
    (1, 2, 0), (1, 1, 3), (1, 3, 3), (0, 2, 3), (0, 1, 0), (0, 3, 0),
)
ORDER = (1, 2, 3, 0)


def dot(a, b):
    return jnp.dot(a, b, preferred_element_type=jnp.float32)


def dot_t(a, b):
    return lax.dot_general(a, b, (((1,), (1,)), ((), ())), preferred_element_type=jnp.float32)


def iota(shape, dim):
    return lax.broadcasted_iota(jnp.int32, shape, dim)


def kernel(
    slot_hbm, len_hbm, table_hbm, ql_hbm, qr_hbm, lat_hbm, rope_hbm,
    ctx_out, log_out,
    slot_s, len_s, table, ql, qr, lat_v, rope_v, rope_f, tab_p, tab_r, idx_v, idx_s,
    stage_l, stage_r, kv, kr, krx, qs, qcat, s_ref, p_ref,
    acc, r0_acc, h_acc, h_st, r1_acc, r1_st, z_out, z_stat, z_in, z_stats, zt, zt_t,
    load_sem, idx_sem, kv_send, kv_recv, kr_send, kr_recv,
    q_send, q_recv, f_send, f_recv, r0_send, r0_recv, r1_send, r1_recv, z_send, z_recv,
):
    pool = lax.axis_index("pool")
    member = lax.axis_index("dcp")
    px, py = pool // SIDE, pool % SIDE
    z, core = member // 2, member % 2

    def wrap(v):
        return lax.rem(v + 2 * SIDE, SIDE)

    def axes(x, y):
        odd = lax.rem(x + y, 2)
        return ((odd, 1 - odd), (1 - odd, odd))

    def shift(x, y, unit, steps):
        return wrap(x + steps * unit[0]), wrap(y + steps * unit[1])

    def group_at(x, y, place):
        other, key = axes(x, y)
        if place == 0:
            gx, gy = x, y
        elif place == 1:
            gx, gy = shift(x, y, other, 2)
        elif place == 2:
            gx, gy = shift(x, y, key, 1)
        else:
            gx, gy = shift(x, y, key, 3)
        return gx * SIDE + gy

    mine = axes(px, py)

    def peer(axis, steps):
        x, y = shift(px, py, mine[axis], steps)
        return (x * SIDE + y, member)

    sibling = (pool, z * 2 + 1 - core)

    def around(steps):
        return (pool, lax.rem(z + steps, RING) * 2 + core)

    loads = [
        pltpu.make_async_copy(source, target, load_sem.at[i])
        for i, (source, target) in enumerate((
            (slot_hbm, slot_s), (len_hbm, len_s), (table_hbm, table), (ql_hbm, ql),
            (qr_hbm, qr), (rope_hbm, rope_v), (lat_hbm, lat_v),
        ))
    ]
    for copy in loads:
        copy.start()

    barrier = pltpu.get_barrier_semaphore()
    greet = [peer(axis, steps) for axis in (0, 1) for steps in (1, 2, 3)]
    greet += [sibling] + [around(steps) for steps in range(1, RING)]
    for device in greet:
        pl.semaphore_signal(barrier, inc=1, device_id=device, device_id_type=MESH)

    for copy in loads[0:3]:
        copy.wait()

    device = pool * 32 + member
    for g in range(16):
        tab_p[pl.ds(g, 1), :] = table[pl.ds(slot_s[g], 1), :] - device * PAGES
    groups = [group_at(px, py, a) for a in range(4)]
    for a in range(4):
        row = table[pl.ds(slot_s[groups[a]], 1), :]
        for b in range(4):
            x, y = shift(px, py, mine[1] if a < 2 else mine[0], b)
            tab_r[pl.ds(4 * a + b, 1), :] = row - ((x * SIDE + y) * 32 + member) * PAGES

    def picks(tab):
        local = jnp.where((tab >= 0) & (tab < PAGES), tab, 64)
        found = []
        for _ in range(CAP):
            first = jnp.min(local, axis=1, keepdims=True)
            found.append(first)
            local = jnp.where(local > first, local, 64)
        return found

    def lanes(values):
        lane = iota((16, 128), 1)
        out = jnp.zeros((16, 128), jnp.int32)
        for j in range(CAP):
            out = jnp.where(lane == j, values[j], out)
        return out

    idx_v[0:16, :] = lanes([jnp.minimum(v, PAGES - 1) for v in picks(tab_p[...])])
    tab = tab_r[...]
    page = iota((16, MAXP), 1)
    quarter = iota((16, 1), 0) // 4
    length = jnp.zeros((16, 1), jnp.int32)
    for a in range(4):
        length = jnp.where(quarter == a, len_s[slot_s[groups[a]]], length)
    counts = []
    for first in picks(tab):
        number = jnp.sum(jnp.where(tab == first, page, 0), axis=1, keepdims=True)
        count = jnp.clip(length - number * TOK, 0, TOK)
        counts.append(jnp.where(first < 64, count, 0))
    idx_v[16:32, :] = lanes(counts)
    to_smem = pltpu.make_async_copy(idx_v, idx_s, idx_sem)
    to_smem.start()

    def parts(shape):
        r = iota(shape, 0)
        return r // HALF, (r // 8) % RING, (r // 2) % 4, r % 2

    for copy in loads[3:5]:
        copy.wait()
    c_, z_, q_, h_ = parts((ROWS, ROWS))
    perm = (iota((ROWS, ROWS), 1) == q_ * 64 + 4 * z_ + 2 * c_ + h_).astype(jnp.bfloat16)
    qcat[0, :, 0:LAT] = dot(perm, ql[...]).astype(jnp.bfloat16)
    rope_rows = qr[...].astype(jnp.float32)
    for i in range(32):
        qs[4 * i : 4 * i + 4, :] = rope_rows[:, 128 * i : 128 * i + 128]
    c_, z_, q_, h_ = parts((ROWS, 128))
    pick = (iota((ROWS, 128), 1) == (2 * z_ + c_) * 4 + q_).astype(jnp.bfloat16)
    pair = dot(pick, qs[...].astype(jnp.bfloat16))
    swapped = jnp.concatenate([pair[:, 64:128], pair[:, 0:64]], axis=1)
    qcat[0, :, LAT : LAT + 128] = jnp.where(
        iota((ROWS, 128), 1) // 64 == h_, pair, swapped
    ).astype(jnp.bfloat16)

    loads[5].wait()
    for i in range(32):
        rope_f[PAGES * i : PAGES * i + PAGES, :] = rope_v[:, 128 * i : 128 * i + 128].astype(
            jnp.float32
        )
    to_smem.wait()
    loads[6].wait()

    def take(group, j):
        slot = idx_s[group, j]
        return lat_v[slot], rope_f[pl.ds(slot, 32, stride=PAGES), :].astype(jnp.bfloat16)

    pl.semaphore_wait(barrier, len(greet))

    half = pl.ds(pl.multiple_of(core * HALF, HALF), HALF)
    rest = pl.ds(pl.multiple_of((1 - core) * HALF, HALF), HALF)
    query = {}
    for steps, place in ((1, 3), (3, 2), (2, 1)):
        query[place] = pltpu.make_async_remote_copy(
            src_ref=qcat.at[0, half],
            dst_ref=qcat.at[place, half],
            send_sem=q_send.at[place],
            recv_sem=q_recv.at[place],
            device_id=peer(0, steps),
            device_id_type=MESH,
        )
        query[place].start()

    sent = {}
    passed = {}

    def pass_queries():
        for place in (2, 3, 1):
            query[place].wait_recv()
            passed[place] = pltpu.make_async_remote_copy(
                src_ref=qcat.at[place, half],
                dst_ref=qcat.at[place, half],
                send_sem=f_send.at[place],
                recv_sem=f_recv.at[place],
                device_id=sibling,
                device_id_type=MESH,
            )
            passed[place].start()

    issued = []
    for i, (axis, steps, place) in enumerate(SENDS):
        tx, ty = shift(px, py, mine[axis], steps)
        group = group_at(tx, ty, place)
        for j in range(CAP):
            latent, rope = take(group, j)
            stage_l[i, j] = latent
            stage_r[i, j] = rope
        source = 4 - steps
        pair_of = (
            pltpu.make_async_remote_copy(
                src_ref=stage_l.at[i],
                dst_ref=kv.at[place, :, source],
                send_sem=kv_send.at[i],
                recv_sem=kv_recv.at[place, source],
                device_id=(tx * SIDE + ty, member),
                device_id_type=MESH,
            ),
            pltpu.make_async_remote_copy(
                src_ref=stage_r.at[i],
                dst_ref=kr.at[place, :, source],
                send_sem=kr_send.at[i],
                recv_sem=kr_recv.at[place, source],
                device_id=(tx * SIDE + ty, member),
                device_id_type=MESH,
            ),
        )
        issued.append(pair_of)
        sent[place, source] = pair_of
        if i < 6:
            for copy in pair_of:
                copy.start()
    for a in range(4):
        for j in range(CAP):
            latent, rope = take(groups[a], j)
            kv[a, j, 0] = latent
            kr[a, j, 0] = rope
    pass_queries()
    for i in range(6):
        for copy in issued[i]:
            copy.wait_send()
        for copy in issued[i + 6]:
            copy.start()

    factor = (QK_NOPE + ROPE) ** (-0.5)
    expand = (iota((256, 128), 0) // 2 == iota((256, 128), 1)).astype(jnp.bfloat16)
    parity = iota((256, 128), 1) // 64 == iota((256, 128), 0) % 2
    within = iota((1, 256), 1) % TOK
    source_of = iota((1, 256), 1) // TOK
    lane = iota((HALF, 128), 1)

    def attend(a):
        for j in range(CAP):
            pairs = kr[a, j].reshape(128, 128)
            krx[...] = jnp.where(parity, dot(expand, pairs), 0.0).astype(jnp.bfloat16)
            keys = kv[a, j].reshape(256, LAT)
            scores = dot_t(qcat[a, :, 0:LAT], keys) + dot_t(qcat[a, :, LAT:], krx[...])
            limit = jnp.zeros((1, 256), jnp.int32)
            for b in range(4):
                limit = jnp.where(source_of == b, idx_s[16 + 4 * a + b, j], limit)
            s_ref[:, 256 * j : 256 * j + 256] = jnp.where(within < limit, scores * factor, NEG)
        for block in range(4):
            rows = slice(64 * block, 64 * block + 64)
            s = s_ref[rows, :]
            top = jnp.maximum(jnp.max(s, axis=1, keepdims=True), EMPTY)
            p = jnp.exp(s - top).astype(jnp.bfloat16)
            p_ref[rows, :] = p
            total = jnp.sum(p.astype(jnp.float32), axis=1, keepdims=True)
            l64 = iota((64, 128), 1)
            acc[a, rows, LAT:] = jnp.where(l64 == 0, top, jnp.where(l64 == 1, total, 0.0))
        acc[a, :, 0:LAT] = dot(p_ref[...], kv[a].reshape(SPAN, LAT))

    def merge(parts_):
        top = functools.reduce(jnp.maximum, [t for _, t, _ in parts_])
        scales = [jnp.exp(t - top) for _, t, _ in parts_]
        total = sum(w * l for w, (_, _, l) in zip(scales, parts_))
        sums = sum(w * v for w, (v, _, _) in zip(scales, parts_))
        return sums, top, total

    exchange, returned = {}, {}

    def swap(a):
        exchange[a] = pltpu.make_async_remote_copy(
            src_ref=acc.at[a, rest],
            dst_ref=r0_acc.at[a],
            send_sem=r0_send.at[a],
            recv_sem=r0_recv.at[a],
            device_id=sibling,
            device_id_type=MESH,
        )
        exchange[a].start()

    def halves(a):
        exchange[a].wait_recv()
        own = acc[a, half, LAT:]
        other = r0_acc[a, :, LAT:]
        return [
            (acc[a, half, 0:LAT], own[:, 0:1], own[:, 1:2]),
            (r0_acc[a, :, 0:LAT], other[:, 0:1], other[:, 1:2]),
        ]

    def encode(part):
        sums, top, total = part
        big = jnp.maximum(jnp.max(jnp.abs(sums), axis=1, keepdims=True), 1e-30)
        steps = jnp.round(sums * (32767.0 / big)).astype(jnp.int32)
        stats = jnp.where(
            lane == 0, top, jnp.where(lane == 1, total, jnp.where(lane == 2, big / 32767.0, 0.0))
        )
        return steps, stats.T

    def give_back(a):
        steps_of, stats = encode(merge(halves(a)))
        h_acc[a - 1] = steps_of.astype(jnp.int16)
        h_st[a - 1] = stats[0:8, :]
        axis, steps = {1: (0, 2), 2: (1, 1), 3: (1, 3)}[a]
        slot = {1: 1, 2: 2, 3: 0}[a]
        returned[a] = [
            pltpu.make_async_remote_copy(
                src_ref=source.at[a - 1],
                dst_ref=target.at[slot],
                send_sem=r1_send.at[slot, k],
                recv_sem=r1_recv.at[slot, k],
                device_id=peer(axis, steps),
                device_id_type=MESH,
            )
            for k, (source, target) in enumerate(((h_st, r1_st), (h_acc, r1_acc)))
        ]
        for copy in returned[a]:
            copy.start()

    pending = None
    for a in ORDER:
        if a:
            passed[a].wait_recv()
        for source in (1, 2, 3):
            for copy in sent[a, source]:
                copy.wait_recv()
        attend(a)
        swap(a)
        if pending is not None:
            give_back(pending)
        pending = a

    pieces = halves(0)
    for a in (1, 2, 3):
        for copy in returned[a]:
            copy.wait_recv()
    for slot in range(3):
        back = jnp.concatenate([r1_st[slot], jnp.zeros((120, 128), jnp.float32)], axis=0).T
        values = r1_acc[slot].astype(jnp.int32).astype(jnp.float32) * back[:, 2:3]
        pieces.append((values, back[:, 0:1], back[:, 1:2]))
    steps_of, stats = encode(merge(pieces))
    blocks = steps_of.reshape(RING, 8, LAT)
    z_out[...] = jnp.concatenate([blocks[:, :, 0:256], blocks[:, :, 256:512]], axis=1).astype(
        jnp.int16
    )
    for k in range(3):
        z_stat[k] = stats[k : k + 1, :]

    spread = []
    for steps in range(1, RING):
        spread.append([
            pltpu.make_async_remote_copy(
                src_ref=source,
                dst_ref=target.at[steps],
                send_sem=z_send.at[steps, k],
                recv_sem=z_recv.at[steps, k],
                device_id=around(steps),
                device_id_type=MESH,
            )
            for k, (source, target) in enumerate((
                (z_stat, z_stats), (z_out.at[lax.rem(z + steps, RING)], z_in),
            ))
        ])
    for k in range(2):
        for copies in spread:
            copies[k].start()
    z_in[0] = z_out[z]
    z_stats[0] = z_stat[...]
    zt[...] = jnp.zeros((128, 128), jnp.float32)
    for i in range(RING):
        if i:
            spread[i - 1][0].wait_recv()
        for k in range(3):
            zt[16 * k + i : 16 * k + i + 1, :] = z_stats[i, k]
    zt_t[...] = zt[...].T
    mine_t = zt_t[pl.ds(pl.multiple_of(z * 8, 8), 8), :]
    tops = mine_t[:, 0:16]
    top = jnp.max(tops, axis=1, keepdims=True)
    weight = jnp.exp(tops - top)
    total = jnp.sum(weight * mine_t[:, 16:32], axis=1, keepdims=True)
    weight = weight * mine_t[:, 32:48] / total
    weight = jnp.concatenate([weight, weight], axis=0)
    log_out[...] = jnp.broadcast_to(top + jnp.log(total), (8, 128))
    context = jnp.zeros((16, 256), jnp.float32)
    for i in range(RING):
        if i:
            spread[i - 1][1].wait_recv()
        context += z_in[i].astype(jnp.int32).astype(jnp.float32) * weight[:, i : i + 1]
    ctx_out[:, 0:256] = context[0:8]
    ctx_out[:, 256:512] = context[8:16]

    for copies in spread:
        for copy in copies:
            copy.wait_send()
    for place in (1, 2, 3):
        query[place].wait_send()
        passed[place].wait_send()
        for copy in returned[place]:
            copy.wait_send()
    for a in range(4):
        exchange[a].wait_send()
    for pair_of in issued[6:]:
        for copy in pair_of:
            copy.wait_send()


def per_device(q_latent, q_rope, pool_latent, pool_rope, page_table, lengths, slot_request):
    vmem = pl.BlockSpec(memory_space=pltpu.VMEM)
    anywhere = pl.BlockSpec(memory_space=pl.ANY)
    f32, bf16, i32, i16 = jnp.float32, jnp.bfloat16, jnp.int32, jnp.int16
    dma = pltpu.SemaphoreType.DMA
    ctx, log = pl.pallas_call(
        kernel,
        out_shape=(jax.ShapeDtypeStruct((8, LAT), f32), jax.ShapeDtypeStruct((8, 128), f32)),
        in_specs=[anywhere] * 7,
        out_specs=(vmem, vmem),
        scratch_shapes=[
            pltpu.SMEM((16,), i32),
            pltpu.SMEM((16,), i32),
            pltpu.VMEM((16, MAXP), i32),
            pltpu.VMEM((ROWS, LAT), bf16),
            pltpu.VMEM((4, 64 * ROPE), bf16),
            pltpu.VMEM((PAGES, TOK, LAT), bf16),
            pltpu.VMEM((PAGES, TOK * ROPE), bf16),
            pltpu.VMEM((32 * PAGES, 128), f32),
            pltpu.VMEM((16, MAXP), i32),
            pltpu.VMEM((16, MAXP), i32),
            pltpu.VMEM((32, 128), i32),
            pltpu.SMEM((32, 128), i32),
            pltpu.VMEM((12, CAP, TOK, LAT), bf16),
            pltpu.VMEM((12, CAP, 32, 128), bf16),
            pltpu.VMEM((4, CAP, 4, TOK, LAT), bf16),
            pltpu.VMEM((4, CAP, 4, 32, 128), bf16),
            pltpu.VMEM((256, 128), bf16),
            pltpu.VMEM((128, 128), f32),
            pltpu.VMEM((4, ROWS, LAT + 128), bf16),
            pltpu.VMEM((ROWS, SPAN), f32),
            pltpu.VMEM((ROWS, SPAN), bf16),
            pltpu.VMEM((4, ROWS, LAT + 128), f32),
            pltpu.VMEM((4, HALF, LAT + 128), f32),
            pltpu.VMEM((3, HALF, LAT), i16),
            pltpu.VMEM((3, 8, 128), f32),
            pltpu.VMEM((3, HALF, LAT), i16),
            pltpu.VMEM((3, 8, 128), f32),
            pltpu.VMEM((RING, 16, 256), i16),
            pltpu.VMEM((3, 1, 128), f32),
            pltpu.VMEM((RING, 16, 256), i16),
            pltpu.VMEM((RING, 3, 1, 128), f32),
            pltpu.VMEM((128, 128), f32),
            pltpu.VMEM((128, 128), f32),
            dma((7,)),
            dma,
            dma((12,)),
            dma((4, 4)),
            dma((12,)),
            dma((4, 4)),
            dma((4,)),
            dma((4,)),
            dma((4,)),
            dma((4,)),
            dma((4,)),
            dma((4,)),
            dma((3, 2)),
            dma((3, 2)),
            dma((RING, 2)),
            dma((RING, 2)),
        ],
        compiler_params=pltpu.CompilerParams(
            collective_id=0, has_side_effects=True, vmem_limit_bytes=60 * 2**20
        ),
        cost_estimate=pl.CostEstimate(flops=2 * 10**9, bytes_accessed=4 * 10**6, transcendentals=10**6),
    )(
        slot_request,
        lengths,
        page_table,
        q_latent.reshape(ROWS, LAT),
        q_rope.reshape(4, 64 * ROPE),
        pool_latent,
        pool_rope,
    )
    context = ctx.astype(bf16).reshape(1, 4, 2, LAT)
    return context, log[:, 0].reshape(1, 4, 2)


def solution(mesh):
    in_specs = (
        P("pool", None, None, None),
        P("pool", None, None),
        P(("pool", "dcp"), None, None),
        P(("pool", "dcp"), None),
        P(),
        P(),
        P(),
    )
    out_specs = (P("pool", None, "dcp", None), P("pool", None, "dcp"))
    return jax.shard_map(
        per_device, mesh=mesh, in_specs=in_specs, out_specs=out_specs, check_vma=False
    )
```

```python
import functools

import jax
import jax.numpy as jnp
from jax import lax
from jax.experimental import pallas as pl
from jax.experimental.pallas import tpu as pltpu
from jax.sharding import PartitionSpec as P

MESH = pl.DeviceIdType.MESH
QK_NOPE = 128
NEG = -1e30
EMPTY = -1e29

SIDE = 4
RING = 16
PAGES = 48
CAP = 3
TOK = 64
LAT = 512
ROPE = 64
ROWS = 256
PART = 64
SPAN = 768
MAXP = 1536

SENDS = (
    (1, 2, 1), (1, 1, 2), (1, 3, 2), (0, 2, 2), (0, 1, 1), (0, 3, 1),
    (1, 1, 3), (1, 3, 3), (0, 2, 3),
    (1, 2, 0), (0, 1, 0), (0, 3, 0),
)
FAR = (8, 7, 9, 6, 10, 5, 11, 4)
NEAR = (12, 3, 13, 2, 14, 1, 15)


def dot(a, b):
    return jnp.dot(a, b, preferred_element_type=jnp.float32)


def dot_t(a, b):
    return lax.dot_general(a, b, (((1,), (1,)), ((), ())), preferred_element_type=jnp.float32)


def iota(shape, dim):
    return lax.broadcasted_iota(jnp.int32, shape, dim)


def kernel(
    slot_hbm, len_hbm, table_hbm, ql_hbm, qr_hbm, lat_hbm, rope_hbm,
    out,
    slot_s, len_s, table, ql, qr, lat_v, rope_v, rope_f, tab_p, tab_r, idx_v, idx_s,
    stage_l, stage_r, kv, kr, krx, qs, qcat, s_ref, p_ref,
    acc, r0_acc, h_acc, h_st, r1_acc, r1_st, z_out, z_stat, z_in, z_stats, zt,
    load_sem, idx_sem, kv_send, kv_recv, kr_send, kr_recv,
    q_send, q_recv, f_send, f_recv, r0_send, r0_recv, r1_send, r1_recv, z_send, z_recv,
):
    pool = lax.axis_index("pool")
    member = lax.axis_index("dcp")
    px, py = pool // SIDE, pool % SIDE
    z, core = member // 2, member % 2

    def wait(ref, sem):
        pltpu.make_async_copy(ref, ref, sem).wait()

    def wrap(v):
        return lax.rem(v + 2 * SIDE, SIDE)

    def axes(x, y):
        odd = lax.rem(x + y, 2)
        return ((odd, 1 - odd), (1 - odd, odd))

    def shift(x, y, unit, steps):
        return wrap(x + steps * unit[0]), wrap(y + steps * unit[1])

    def group_at(x, y, place):
        other, key = axes(x, y)
        if place == 0:
            gx, gy = x, y
        elif place == 1:
            gx, gy = shift(x, y, other, 2)
        elif place == 2:
            gx, gy = shift(x, y, key, 1)
        else:
            gx, gy = shift(x, y, key, 3)
        return gx * SIDE + gy

    mine = axes(px, py)

    def peer(axis, steps):
        x, y = shift(px, py, mine[axis], steps)
        return (x * SIDE + y, member)

    sibling = (pool, z * 2 + 1 - core)

    def around(steps):
        return (pool, lax.rem(z + steps, RING) * 2 + core)

    loads = [
        pltpu.make_async_copy(source, target, load_sem.at[i])
        for i, (source, target) in enumerate((
            (slot_hbm, slot_s), (len_hbm, len_s), (table_hbm, table), (ql_hbm, ql),
            (qr_hbm, qr), (rope_hbm, rope_v), (lat_hbm, lat_v),
        ))
    ]
    for copy in loads:
        copy.start()

    barrier = pltpu.get_barrier_semaphore()
    greet = [peer(axis, steps) for axis in (0, 1) for steps in (1, 2, 3)]
    greet += [sibling] + [around(steps) for steps in range(1, RING)]
    for device in greet:
        pl.semaphore_signal(barrier, inc=1, device_id=device, device_id_type=MESH)

    for copy in loads[0:3]:
        copy.wait()

    device = pool * 32 + member
    for g in range(16):
        tab_p[pl.ds(g, 1), :] = table[pl.ds(slot_s[g], 1), :] - device * PAGES
    groups = [group_at(px, py, a) for a in range(4)]
    for a in range(4):
        row = table[pl.ds(slot_s[groups[a]], 1), :]
        for b in range(4):
            x, y = shift(px, py, mine[1] if a < 2 else mine[0], b)
            tab_r[pl.ds(4 * a + b, 1), :] = row - ((x * SIDE + y) * 32 + member) * PAGES

    def picks(tab):
        local = jnp.where((tab >= 0) & (tab < PAGES), tab, 64)
        found = []
        for _ in range(CAP):
            first = jnp.min(local, axis=1, keepdims=True)
            found.append(first)
            local = jnp.where(local > first, local, 64)
        return found

    def lanes(values):
        lane = iota((16, 128), 1)
        out = jnp.zeros((16, 128), jnp.int32)
        for j in range(CAP):
            out = jnp.where(lane == j, values[j], out)
        return out

    idx_v[0:16, :] = lanes([jnp.minimum(v, PAGES - 1) for v in picks(tab_p[...])])
    tab = tab_r[...]
    page = iota((16, MAXP), 1)
    quarter = iota((16, 1), 0) // 4
    length = jnp.zeros((16, 1), jnp.int32)
    for a in range(4):
        length = jnp.where(quarter == a, len_s[slot_s[groups[a]]], length)
    counts = []
    for first in picks(tab):
        number = jnp.sum(jnp.where(tab == first, page, 0), axis=1, keepdims=True)
        count = jnp.clip(length - number * TOK, 0, TOK)
        counts.append(jnp.where(first < 64, count, 0))
    idx_v[16:32, :] = lanes(counts)
    to_smem = pltpu.make_async_copy(idx_v, idx_s, idx_sem)
    to_smem.start()

    def parts(shape):
        r = iota(shape, 0)
        steps = (r // 128) * 8 + 4 + (r // 8) % 8
        return (r // PART) % 2, (z + steps) % RING, (r // 2) % 4, r % 2

    for copy in loads[3:5]:
        copy.wait()
    c_, z_, q_, h_ = parts((ROWS, ROWS))
    perm = (iota((ROWS, ROWS), 1) == q_ * 64 + 4 * z_ + 2 * c_ + h_).astype(jnp.bfloat16)

    def split(rows):
        return rows.astype(jnp.bfloat16).reshape(2, 2, PART, -1)

    qcat[0, :, :, :, 0:LAT] = split(dot(perm, ql[...]))
    rope_rows = qr[...].astype(jnp.float32)
    for i in range(32):
        qs[4 * i : 4 * i + 4, :] = rope_rows[:, 128 * i : 128 * i + 128]
    c_, z_, q_, h_ = parts((ROWS, 128))
    pick = (iota((ROWS, 128), 1) == (2 * z_ + c_) * 4 + q_).astype(jnp.bfloat16)
    pair = dot(pick, qs[...].astype(jnp.bfloat16))
    swapped = jnp.concatenate([pair[:, 64:128], pair[:, 0:64]], axis=1)
    qcat[0, :, :, :, LAT:] = split(jnp.where(iota((ROWS, 128), 1) // 64 == h_, pair, swapped))

    to_smem.wait()
    pl.semaphore_wait(barrier, len(greet))

    query = {}
    for steps, place in ((1, 3), (3, 2), (2, 1)):
        query[place] = pltpu.make_async_remote_copy(
            src_ref=qcat.at[0, :, core],
            dst_ref=qcat.at[place, :, core],
            send_sem=q_send,
            recv_sem=q_recv.at[place],
            device_id=peer(0, steps),
            device_id_type=MESH,
        )
        query[place].start()

    loads[5].wait()
    for i in range(32):
        rope_f[PAGES * i : PAGES * i + PAGES, :] = rope_v[:, 128 * i : 128 * i + 128].astype(
            jnp.float32
        )
    loads[6].wait()

    def take(group, j):
        slot = idx_s[group, j]
        return lat_v[slot], rope_f[pl.ds(slot, 32, stride=PAGES), :].astype(jnp.bfloat16)

    passed = {}

    def pass_queries():
        for place in (2, 3, 1):
            query[place].wait_recv()
            passed[place] = pltpu.make_async_remote_copy(
                src_ref=qcat.at[place, :, core],
                dst_ref=qcat.at[place, :, core],
                send_sem=f_send,
                recv_sem=f_recv.at[place],
                device_id=sibling,
                device_id_type=MESH,
            )
            passed[place].start()

    def pack(i):
        axis, steps, place = SENDS[i]
        group = group_at(*shift(px, py, mine[axis], steps), place)
        for j in range(CAP):
            latent, rope = take(group, j)
            stage_l[i, j] = latent
            stage_r[i, j] = rope

    def send(i):
        axis, steps, place = SENDS[i]
        for source, target, sends, recvs in (
            (stage_l, kv, kv_send, kv_recv), (stage_r, kr, kr_send, kr_recv),
        ):
            pltpu.make_async_remote_copy(
                src_ref=source.at[i],
                dst_ref=target.at[place, :, 4 - steps],
                send_sem=sends,
                recv_sem=recvs.at[place],
                device_id=peer(axis, steps),
                device_id_type=MESH,
            ).start()

    for i in range(12):
        pack(i)
        send(i)
    pass_queries()
    for a in range(4):
        for j in range(CAP):
            latent, rope = take(groups[a], j)
            kv[a, j, 0] = latent
            kr[a, j, 0] = rope

    factor = (QK_NOPE + ROPE) ** (-0.5)
    expand = (iota((256, 128), 0) // 2 == iota((256, 128), 1)).astype(jnp.bfloat16)
    parity = iota((256, 128), 1) // 64 == iota((256, 128), 0) % 2
    within = iota((1, 256), 1) % TOK
    source_of = iota((1, 256), 1) // TOK
    lane = iota((128, 128), 1)

    def expand_keys(a):
        for j in range(CAP):
            pairs = kr[a, j].reshape(128, 128)
            krx[a, 256 * j : 256 * j + 256, :] = jnp.where(
                parity, dot(expand, pairs), 0.0
            ).astype(jnp.bfloat16)

    def attend(a, k):
        rows_l = qcat[a, k, :, :, 0:LAT].reshape(128, LAT)
        rows_r = qcat[a, k, :, :, LAT:].reshape(128, 128)
        for j in range(CAP):
            keys = kv[a, j].reshape(256, LAT)
            scores = dot_t(rows_l, keys) + dot_t(rows_r, krx[a, 256 * j : 256 * j + 256, :])
            limit = jnp.zeros((1, 256), jnp.int32)
            for b in range(4):
                limit = jnp.where(source_of == b, idx_s[16 + 4 * a + b, j], limit)
            s_ref[:, 256 * j : 256 * j + 256] = jnp.where(within < limit, scores * factor, NEG)
        for c in range(2):
            rows = slice(PART * c, PART * c + PART)
            s = s_ref[rows, :]
            top = jnp.maximum(jnp.max(s, axis=1, keepdims=True), EMPTY)
            p = jnp.exp(s - top).astype(jnp.bfloat16)
            p_ref[rows, :] = p
            total = jnp.sum(p.astype(jnp.float32), axis=1, keepdims=True)
            acc[a, k, c, :, LAT:] = jnp.where(
                lane[0:PART] == 0, top, jnp.where(lane[0:PART] == 1, total, 0.0)
            )
        acc[a, k, :, :, 0:LAT] = dot(p_ref[...], kv[a].reshape(SPAN, LAT)).reshape(2, PART, LAT)

    def merge(parts_):
        top = functools.reduce(jnp.maximum, [t for _, t, _ in parts_])
        scales = [jnp.exp(t - top) for _, t, _ in parts_]
        total = sum(w * l for w, (_, _, l) in zip(scales, parts_))
        sums = sum(w * v for w, (v, _, _) in zip(scales, parts_))
        return sums, top, total

    exchange = {}

    def swap(a, k):
        exchange[a, k] = pltpu.make_async_remote_copy(
            src_ref=acc.at[a, k, 1 - core],
            dst_ref=r0_acc.at[a, k],
            send_sem=r0_send,
            recv_sem=r0_recv.at[a, k],
            device_id=sibling,
            device_id_type=MESH,
        )
        exchange[a, k].start()

    def halves(a, k):
        exchange[a, k].wait_recv()
        own = acc[a, k, core]
        other = r0_acc[a, k]
        return [(v[:, 0:LAT], v[:, LAT : LAT + 1], v[:, LAT + 1 : LAT + 2]) for v in (own, other)]

    def encode(part):
        sums, top, total = part
        big = jnp.maximum(jnp.max(jnp.abs(sums), axis=1, keepdims=True), 1e-30)
        steps = jnp.round(sums * (32767.0 / big)).astype(jnp.int32)
        first = jnp.concatenate([top, total], axis=0)
        second = jnp.concatenate([big / 32767.0, big], axis=0)
        stats = jnp.where(lane == 0, first, jnp.where(lane == 1, second, 0.0)).T
        return steps, stats

    def give_back(a, k):
        steps_of, stats = encode(merge(halves(a, k)))
        h_acc[a - 1, k] = steps_of.astype(jnp.int16)
        h_st[a - 1, k] = stats[0:8, :]
        axis, steps = {1: (0, 2), 2: (1, 1), 3: (1, 3)}[a]
        slot = {1: 1, 2: 2, 3: 0}[a]
        for n, (source, target) in enumerate(((h_st, r1_st), (h_acc, r1_acc))):
            pltpu.make_async_remote_copy(
                src_ref=source.at[a - 1, k],
                dst_ref=target.at[k, slot],
                send_sem=r1_send.at[n],
                recv_sem=r1_recv.at[k, n],
                device_id=peer(axis, steps),
                device_id_type=MESH,
            ).start()

    def finish(k):
        pieces = halves(0, k)
        for n, target in enumerate((r1_st, r1_acc)):
            wait(target.at[k], r1_recv.at[k, n])
        for slot in range(3):
            back = jnp.concatenate([r1_st[k, slot], jnp.zeros((120, 128), jnp.float32)], axis=0).T
            values = r1_acc[k, slot].astype(jnp.int32).astype(jnp.float32) * back[0:PART, 1:2]
            pieces.append((values, back[0:PART, 0:1], back[PART:, 0:1]))
        steps_of, stats = encode(merge(pieces))
        blocks = steps_of.reshape(8, 8, LAT)
        z_out[k] = jnp.concatenate([blocks[:, :, 0:256], blocks[:, :, 256:512]], axis=1).astype(
            jnp.int16
        )
        for n in range(2):
            z_stat[k, n] = stats[n : n + 1, :]
        for n in range(2):
            for steps in (FAR, NEAR)[k]:
                copy = pltpu.make_async_remote_copy(
                    src_ref=(z_stat.at[k], z_out.at[k, (steps + 4) % 8])[n],
                    dst_ref=(z_stats, z_in)[n].at[steps],
                    send_sem=z_send.at[n],
                    recv_sem=z_recv.at[n],
                    device_id=around(steps),
                    device_id_type=MESH,
                )
                copy.start()

    for a in (1, 2, 3, 0):
        if a:
            passed[a].wait_recv()
        wait(kv.at[a, :, 1:4], kv_recv.at[a])
        wait(kr.at[a, :, 1:4], kr_recv.at[a])
        expand_keys(a)
        for k in range(2):
            attend(a, k)
            swap(a, k)
        if a:
            give_back(a, 0)
            give_back(a, 1)
    finish(0)
    finish(1)

    z_in[0] = z_out[1, 4]
    z_stats[0] = z_stat[1]
    zt[...] = jnp.zeros((128, 128), jnp.float32)
    wait(z_stats.at[1:RING], z_recv.at[0])
    for i in range(RING):
        for n in range(2):
            zt[16 * n + i : 16 * n + i + 1, :] = z_stats[i, n]
    turned = zt[...].T
    which = (iota((8, 128), 1) % 16 + 4) % 8
    tops = jnp.zeros((8, 128), jnp.float32)
    totals = tops
    for j in range(8):
        tops = jnp.where(which == j, turned[8 * j : 8 * j + 8], tops)
        totals = jnp.where(which == j, turned[PART + 8 * j : PART + 8 * j + 8], totals)
    sizes, tops, totals = tops[:, 16:32], tops[:, 0:16], totals[:, 0:16]
    top = jnp.max(tops, axis=1, keepdims=True)
    weight = jnp.exp(tops - top)
    total = jnp.sum(weight * totals, axis=1, keepdims=True)
    weight = weight * sizes / total
    weight = jnp.concatenate([weight, weight], axis=0)
    context = jnp.zeros((16, 256), jnp.float32)
    wait(z_in.at[1:RING], z_recv.at[1])
    for i in range(RING):
        context += z_in[i].astype(jnp.int32).astype(jnp.float32) * weight[:, i : i + 1]
    out[:, 0:256] = context[0:8]
    out[:, 256:512] = context[8:16]
    out[:, 512:] = jnp.broadcast_to(top + jnp.log(total), (8, 128))

    wait(z_stats.at[1:RING], z_send.at[0])
    wait(z_in.at[1:RING], z_send.at[1])
    wait(qcat.at[1:4, :, 0], q_send)
    wait(qcat.at[1:4, :, 0], f_send)
    wait(stage_l, kv_send)
    wait(stage_r, kr_send)
    wait(r0_acc, r0_send)
    wait(h_st, r1_send.at[0])
    wait(h_acc, r1_send.at[1])


def layout_kernel(rows, ctx_out, log_out):
    for q in range(4):
        ctx_out[q] = rows[2 * q : 2 * q + 2, 0:LAT].astype(jnp.bfloat16)
    cell, spot = iota((8, 128), 0), iota((8, 128), 1)
    for h in range(2):
        line = jnp.where((cell % 2 == h) & (spot == cell // 2), rows[:, LAT:], 0.0)
        log_out[h : h + 1, :] = jnp.sum(line, axis=0, keepdims=True)[:, 0:4]


def per_device(q_latent, q_rope, pool_latent, pool_rope, page_table, lengths, slot_request):
    vmem = pl.BlockSpec(memory_space=pltpu.VMEM)
    anywhere = pl.BlockSpec(memory_space=pl.ANY)
    f32, bf16, i32, i16 = jnp.float32, jnp.bfloat16, jnp.int32, jnp.int16
    dma = pltpu.SemaphoreType.DMA
    rows = pl.pallas_call(
        kernel,
        out_shape=jax.ShapeDtypeStruct((8, LAT + 128), f32),
        in_specs=[anywhere] * 7,
        out_specs=vmem,
        scratch_shapes=[
            pltpu.SMEM((16,), i32),
            pltpu.SMEM((16,), i32),
            pltpu.VMEM((16, MAXP), i32),
            pltpu.VMEM((ROWS, LAT), bf16),
            pltpu.VMEM((4, 64 * ROPE), bf16),
            pltpu.VMEM((PAGES, TOK, LAT), bf16),
            pltpu.VMEM((PAGES, TOK * ROPE), bf16),
            pltpu.VMEM((32 * PAGES, 128), f32),
            pltpu.VMEM((16, MAXP), i32),
            pltpu.VMEM((16, MAXP), i32),
            pltpu.VMEM((32, 128), i32),
            pltpu.SMEM((32, 128), i32),
            pltpu.VMEM((12, CAP, TOK, LAT), bf16),
            pltpu.VMEM((12, CAP, 32, 128), bf16),
            pltpu.VMEM((4, CAP, 4, TOK, LAT), bf16),
            pltpu.VMEM((4, CAP, 4, 32, 128), bf16),
            pltpu.VMEM((4, SPAN, 128), bf16),
            pltpu.VMEM((128, 128), f32),
            pltpu.VMEM((4, 2, 2, PART, LAT + 128), bf16),
            pltpu.VMEM((128, SPAN), f32),
            pltpu.VMEM((128, SPAN), bf16),
            pltpu.VMEM((4, 2, 2, PART, LAT + 128), f32),
            pltpu.VMEM((4, 2, PART, LAT + 128), f32),
            pltpu.VMEM((3, 2, PART, LAT), i16),
            pltpu.VMEM((3, 2, 8, 128), f32),
            pltpu.VMEM((2, 3, PART, LAT), i16),
            pltpu.VMEM((2, 3, 8, 128), f32),
            pltpu.VMEM((2, 8, 16, 256), i16),
            pltpu.VMEM((2, 2, 1, 128), f32),
            pltpu.VMEM((RING, 16, 256), i16),
            pltpu.VMEM((RING, 2, 1, 128), f32),
            pltpu.VMEM((128, 128), f32),
            dma((7,)),
            dma,
            dma,
            dma((4,)),
            dma,
            dma((4,)),
            dma,
            dma((4,)),
            dma,
            dma((4,)),
            dma,
            dma((4, 2)),
            dma((2,)),
            dma((2, 2)),
            dma((2,)),
            dma((2,)),
        ],
        compiler_params=pltpu.CompilerParams(
            collective_id=0, has_side_effects=True, vmem_limit_bytes=60 * 2**20
        ),
        cost_estimate=pl.CostEstimate(flops=2 * 10**9, bytes_accessed=4 * 10**6, transcendentals=10**6),
    )(
        slot_request,
        lengths,
        page_table,
        q_latent.reshape(ROWS, LAT),
        q_rope.reshape(4, 64 * ROPE),
        pool_latent,
        pool_rope,
    )
    ctx, log = pl.pallas_call(
        layout_kernel,
        out_shape=(jax.ShapeDtypeStruct((4, 2, LAT), bf16), jax.ShapeDtypeStruct((2, 4), f32)),
        in_specs=[vmem],
        out_specs=(vmem, vmem),
        compiler_params=pltpu.CompilerParams(vmem_limit_bytes=60 * 2**20),
    )(rows)
    return ctx.reshape(1, 4, 2, LAT), log.T.reshape(1, 4, 2)


def solution(mesh):
    in_specs = (
        P("pool", None, None, None),
        P("pool", None, None),
        P(("pool", "dcp"), None, None),
        P(("pool", "dcp"), None),
        P(),
        P(),
        P(),
    )
    out_specs = (P("pool", None, "dcp", None), P("pool", None, "dcp"))
    return jax.shard_map(
        per_device, mesh=mesh, in_specs=in_specs, out_specs=out_specs, check_vma=False
    )
```

```python
import functools

import jax
import jax.numpy as jnp
from jax import lax
from jax.experimental import pallas as pl
from jax.experimental.pallas import tpu as pltpu
from jax.sharding import PartitionSpec as P

MESH = pl.DeviceIdType.MESH
QK_NOPE = 128
NEG = -1e30
EMPTY = -1e29

SIDE = 4
RING = 16
PAGES = 48
CAP = 3
TOK = 64
LAT = 512
ROPE = 64
ROWS = 256
PART = 64
SPAN = 768
MAXP = 1536

SENDS = (
    (1, 2, 1), (0, 2, 2), (1, 1, 2), (1, 3, 2), (0, 1, 1), (0, 3, 1), (0, 2, 3), (1, 1, 3), (1, 3, 3), (1, 2, 0), (0, 1, 0), (0, 3, 0),
)
FAR = (8, 7, 9, 6, 10, 5, 11, 4)
NEAR = (12, 3, 13, 2, 14, 1, 15)


def dot(a, b):
    return jnp.dot(a, b, preferred_element_type=jnp.float32)


def dot_t(a, b):
    return lax.dot_general(a, b, (((1,), (1,)), ((), ())), preferred_element_type=jnp.float32)


def iota(shape, dim):
    return lax.broadcasted_iota(jnp.int32, shape, dim)


def kernel(
    slot_hbm, len_hbm, table_hbm, ql_hbm, qr_hbm, lat_hbm, rope_hbm,
    out,
    slot_s, len_s, table, ql, qr, lat_v, rope_v, rope_f, tab_p, tab_r, idx_v, idx_s,
    stage_l, stage_r, kv, kr, krx, qs, qcat, s_ref, p_ref,
    acc, r0_acc, h_acc, h_st, r1_acc, r1_st, z_out, z_stat, z_in, z_stats, zt,
    load_sem, idx_sem, kv_send, kv_recv, kr_send, kr_recv,
    q_send, q_recv, f_send, f_recv, r0_send, r0_recv, r1_send, r1_recv, z_send, z_recv,
):
    pool = lax.axis_index("pool")
    member = lax.axis_index("dcp")
    px, py = pool // SIDE, pool % SIDE
    z, core = member // 2, member % 2

    def wait(ref, sem):
        pltpu.make_async_copy(ref, ref, sem).wait()

    def wrap(v):
        return lax.rem(v + 2 * SIDE, SIDE)

    def axes(x, y):
        odd = lax.rem(x + y, 2)
        return ((odd, 1 - odd), (1 - odd, odd))

    def shift(x, y, unit, steps):
        return wrap(x + steps * unit[0]), wrap(y + steps * unit[1])

    def group_at(x, y, place):
        other, key = axes(x, y)
        if place == 0:
            gx, gy = x, y
        elif place == 1:
            gx, gy = shift(x, y, other, 2)
        elif place == 2:
            gx, gy = shift(x, y, key, 1)
        else:
            gx, gy = shift(x, y, key, 3)
        return gx * SIDE + gy

    mine = axes(px, py)

    def peer(axis, steps):
        x, y = shift(px, py, mine[axis], steps)
        return (x * SIDE + y, member)

    sibling = (pool, z * 2 + 1 - core)

    def around(steps):
        return (pool, lax.rem(z + steps, RING) * 2 + core)

    loads = [
        pltpu.make_async_copy(source, target, load_sem.at[i])
        for i, (source, target) in enumerate((
            (slot_hbm, slot_s), (len_hbm, len_s), (table_hbm, table), (ql_hbm, ql),
            (qr_hbm, qr), (rope_hbm, rope_v), (lat_hbm, lat_v),
        ))
    ]
    for copy in loads:
        copy.start()

    barrier = pltpu.get_barrier_semaphore()
    greet = [peer(axis, steps) for axis in (0, 1) for steps in (1, 2, 3)]
    greet += [sibling] + [around(steps) for steps in range(1, RING)]
    for device in greet:
        pl.semaphore_signal(barrier, inc=1, device_id=device, device_id_type=MESH)

    def parts(shape):
        r = iota(shape, 0)
        steps = (r // 128) * 8 + 4 + (r // 8) % 8
        return (r // PART) % 2, (z + steps) % RING, (r // 2) % 4, r % 2

    for copy in loads[3:5]:
        copy.wait()
    c_, z_, q_, h_ = parts((ROWS, ROWS))
    perm = (iota((ROWS, ROWS), 1) == q_ * 64 + 4 * z_ + 2 * c_ + h_).astype(jnp.bfloat16)

    def split(rows):
        return rows.astype(jnp.bfloat16).reshape(2, 2, PART, -1)

    qcat[0, :, :, :, 0:LAT] = split(dot(perm, ql[...]))
    rope_rows = qr[...].astype(jnp.float32)
    for i in range(32):
        qs[4 * i : 4 * i + 4, :] = rope_rows[:, 128 * i : 128 * i + 128]
    c_, z_, q_, h_ = parts((ROWS, 128))
    pick = (iota((ROWS, 128), 1) == (2 * z_ + c_) * 4 + q_).astype(jnp.bfloat16)
    pair = dot(pick, qs[...].astype(jnp.bfloat16))
    swapped = jnp.concatenate([pair[:, 64:128], pair[:, 0:64]], axis=1)
    qcat[0, :, :, :, LAT:] = split(jnp.where(iota((ROWS, 128), 1) // 64 == h_, pair, swapped))

    pl.semaphore_wait(barrier, len(greet))

    query = {}
    for steps, place in ((2, 1), (1, 3), (3, 2)):
        query[place] = pltpu.make_async_remote_copy(
            src_ref=qcat.at[0, :, core],
            dst_ref=qcat.at[place, :, core],
            send_sem=q_send,
            recv_sem=q_recv.at[place],
            device_id=peer(0, steps),
            device_id_type=MESH,
        )
        query[place].start()

    for copy in loads[0:3]:
        copy.wait()

    device = pool * 32 + member
    for g in range(16):
        tab_p[pl.ds(g, 1), :] = table[pl.ds(slot_s[g], 1), :] - device * PAGES
    groups = [group_at(px, py, a) for a in range(4)]
    for a in range(4):
        row = table[pl.ds(slot_s[groups[a]], 1), :]
        for b in range(4):
            x, y = shift(px, py, mine[1] if a < 2 else mine[0], b)
            tab_r[pl.ds(4 * a + b, 1), :] = row - ((x * SIDE + y) * 32 + member) * PAGES

    def picks(tab):
        local = jnp.where((tab >= 0) & (tab < PAGES), tab, 64)
        found = []
        for _ in range(CAP):
            first = jnp.min(local, axis=1, keepdims=True)
            found.append(first)
            local = jnp.where(local > first, local, 64)
        return found

    def lanes(values):
        lane = iota((16, 128), 1)
        out = jnp.zeros((16, 128), jnp.int32)
        for j in range(CAP):
            out = jnp.where(lane == j, values[j], out)
        return out

    idx_v[0:16, :] = lanes([jnp.minimum(v, PAGES - 1) for v in picks(tab_p[...])])
    tab = tab_r[...]
    page = iota((16, MAXP), 1)
    quarter = iota((16, 1), 0) // 4
    length = jnp.zeros((16, 1), jnp.int32)
    for a in range(4):
        length = jnp.where(quarter == a, len_s[slot_s[groups[a]]], length)
    counts = []
    for first in picks(tab):
        number = jnp.sum(jnp.where(tab == first, page, 0), axis=1, keepdims=True)
        count = jnp.clip(length - number * TOK, 0, TOK)
        counts.append(jnp.where(first < 64, count, 0))
    idx_v[16:32, :] = lanes(counts)
    to_smem = pltpu.make_async_copy(idx_v, idx_s, idx_sem)
    to_smem.start()


    loads[5].wait()
    for i in range(32):
        rope_f[PAGES * i : PAGES * i + PAGES, :] = rope_v[:, 128 * i : 128 * i + 128].astype(
            jnp.float32
        )
    to_smem.wait()
    loads[6].wait()

    def take(group, j):
        slot = idx_s[group, j]
        return lat_v[slot], rope_f[pl.ds(slot, 32, stride=PAGES), :].astype(jnp.bfloat16)

    passed = {}

    def pass_queries():
        for place in (2, 3, 1):
            query[place].wait_recv()
            passed[place] = pltpu.make_async_remote_copy(
                src_ref=qcat.at[place, :, core],
                dst_ref=qcat.at[place, :, core],
                send_sem=f_send,
                recv_sem=f_recv.at[place],
                device_id=sibling,
                device_id_type=MESH,
            )
            passed[place].start()

    def pack(i):
        axis, steps, place = SENDS[i]
        group = group_at(*shift(px, py, mine[axis], steps), place)
        for j in range(CAP):
            latent, rope = take(group, j)
            stage_l[i, j] = latent
            stage_r[i, j] = rope

    def send(i):
        axis, steps, place = SENDS[i]
        for source, target, sends, recvs in (
            (stage_l, kv, kv_send, kv_recv), (stage_r, kr, kr_send, kr_recv),
        ):
            pltpu.make_async_remote_copy(
                src_ref=source.at[i],
                dst_ref=target.at[place, :, 4 - steps],
                send_sem=sends,
                recv_sem=recvs.at[place],
                device_id=peer(axis, steps),
                device_id_type=MESH,
            ).start()

    for i in range(12):
        pack(i)
        send(i)
    pass_queries()
    for a in range(4):
        for j in range(CAP):
            latent, rope = take(groups[a], j)
            kv[a, j, 0] = latent
            kr[a, j, 0] = rope

    factor = (QK_NOPE + ROPE) ** (-0.5)
    expand = (iota((256, 128), 0) // 2 == iota((256, 128), 1)).astype(jnp.bfloat16)
    parity = iota((256, 128), 1) // 64 == iota((256, 128), 0) % 2
    within = iota((1, 256), 1) % TOK
    source_of = iota((1, 256), 1) // TOK
    lane = iota((128, 128), 1)

    def expand_keys(a):
        for j in range(CAP):
            pairs = kr[a, j].reshape(128, 128)
            krx[a, 256 * j : 256 * j + 256, :] = jnp.where(
                parity, dot(expand, pairs), 0.0
            ).astype(jnp.bfloat16)

    def attend(a, k):
        rows_l = qcat[a, k, :, :, 0:LAT].reshape(128, LAT)
        rows_r = qcat[a, k, :, :, LAT:].reshape(128, 128)
        for j in range(CAP):
            keys = kv[a, j].reshape(256, LAT)
            scores = dot_t(rows_l, keys) + dot_t(rows_r, krx[a, 256 * j : 256 * j + 256, :])
            limit = jnp.zeros((1, 256), jnp.int32)
            for b in range(4):
                limit = jnp.where(source_of == b, idx_s[16 + 4 * a + b, j], limit)
            s_ref[:, 256 * j : 256 * j + 256] = jnp.where(within < limit, scores * factor, NEG)
        for c in range(2):
            rows = slice(PART * c, PART * c + PART)
            s = s_ref[rows, :]
            top = jnp.maximum(jnp.max(s, axis=1, keepdims=True), EMPTY)
            p = jnp.exp(s - top).astype(jnp.bfloat16)
            p_ref[rows, :] = p
            total = jnp.sum(p.astype(jnp.float32), axis=1, keepdims=True)
            acc[a, k, c, :, LAT:] = jnp.where(
                lane[0:PART] == 0, top, jnp.where(lane[0:PART] == 1, total, 0.0)
            )
        acc[a, k, :, :, 0:LAT] = dot(p_ref[...], kv[a].reshape(SPAN, LAT)).reshape(2, PART, LAT)

    def merge(parts_):
        top = functools.reduce(jnp.maximum, [t for _, t, _ in parts_])
        scales = [jnp.exp(t - top) for _, t, _ in parts_]
        total = sum(w * l for w, (_, _, l) in zip(scales, parts_))
        sums = sum(w * v for w, (v, _, _) in zip(scales, parts_))
        return sums, top, total

    exchange = {}

    def swap(a, k):
        exchange[a, k] = pltpu.make_async_remote_copy(
            src_ref=acc.at[a, k, 1 - core],
            dst_ref=r0_acc.at[a, k],
            send_sem=r0_send,
            recv_sem=r0_recv.at[a, k],
            device_id=sibling,
            device_id_type=MESH,
        )
        exchange[a, k].start()

    def halves(a, k):
        exchange[a, k].wait_recv()
        own = acc[a, k, core]
        other = r0_acc[a, k]
        return [(v[:, 0:LAT], v[:, LAT : LAT + 1], v[:, LAT + 1 : LAT + 2]) for v in (own, other)]

    def encode(part):
        sums, top, total = part
        big = jnp.maximum(jnp.max(jnp.abs(sums), axis=1, keepdims=True), 1e-30)
        steps = jnp.round(sums * (32767.0 / big)).astype(jnp.int32)
        at, row = iota((PART, 128), 1), iota((PART, 128), 0)
        first = jnp.where(at == row, top, jnp.where(at == row + PART, total, 0.0))
        second = jnp.where(at == row, big * (1.0 / 32767.0), 0.0)
        return steps, [jnp.sum(v, axis=0, keepdims=True) for v in (first, second)]

    def give_back(a, k):
        steps_of, stats = encode(merge(halves(a, k)))
        h_acc[a - 1, k] = steps_of.astype(jnp.int16)
        row = iota((8, 128), 0)
        h_st[a - 1, k] = jnp.where(row == 0, stats[0], jnp.where(row == 1, stats[1], 0.0))
        axis, steps = {1: (0, 2), 2: (1, 1), 3: (1, 3)}[a]
        slot = {1: 1, 2: 2, 3: 0}[a]
        for n, (source, target) in enumerate(((h_st, r1_st), (h_acc, r1_acc))):
            pltpu.make_async_remote_copy(
                src_ref=source.at[a - 1, k],
                dst_ref=target.at[k, slot],
                send_sem=r1_send.at[n],
                recv_sem=r1_recv.at[k, n],
                device_id=peer(axis, steps),
                device_id_type=MESH,
            ).start()

    def finish(k):
        pieces = halves(0, k)
        for n, target in enumerate((r1_st, r1_acc)):
            wait(target.at[k], r1_recv.at[k, n])
        back = r1_st[k].reshape(24, 128)
        back = jnp.concatenate([back, jnp.zeros((104, 128), jnp.float32)], axis=0).T
        for slot in range(3):
            i = 8 * slot
            values = r1_acc[k, slot].astype(jnp.int32).astype(jnp.float32)
            values = values * back[0:PART, i + 1 : i + 2]
            pieces.append((values, back[0:PART, i : i + 1], back[PART:, i : i + 1]))
        steps_of, stats = encode(merge(pieces))
        blocks = steps_of.reshape(8, 8, LAT)
        z_out[k] = jnp.concatenate([blocks[:, :, 0:256], blocks[:, :, 256:512]], axis=1).astype(
            jnp.int16
        )
        for n in range(2):
            z_stat[k, n] = stats[n]
        for n in range(2):
            for steps in (FAR, NEAR)[k]:
                copy = pltpu.make_async_remote_copy(
                    src_ref=(z_stat.at[k], z_out.at[k, (steps + 4) % 8])[n],
                    dst_ref=(z_stats, z_in)[n].at[steps],
                    send_sem=z_send.at[n],
                    recv_sem=z_recv.at[n],
                    device_id=around(steps),
                    device_id_type=MESH,
                )
                copy.start()

    def arrived(a):
        if a:
            passed[a].wait_recv()
        wait(kv.at[a, :, 1:4], kv_recv.at[a])
        wait(kr.at[a, :, 1:4], kr_recv.at[a])
        expand_keys(a)

    def both(a):
        arrived(a)
        for k in range(2):
            attend(a, k)
            swap(a, k)

    both(1)
    give_back(1, 0)
    both(2)
    give_back(2, 0)
    both(3)
    give_back(3, 0)
    arrived(0)
    attend(0, 0)
    swap(0, 0)
    give_back(1, 1)
    give_back(2, 1)
    give_back(3, 1)
    attend(0, 1)
    swap(0, 1)
    finish(0)
    finish(1)

    z_in[0] = z_out[1, 4]
    z_stats[0] = z_stat[1]
    zt[...] = jnp.zeros((128, 128), jnp.float32)
    wait(z_stats.at[1:RING], z_recv.at[0])
    for i in range(RING):
        for n in range(2):
            zt[16 * n + i : 16 * n + i + 1, :] = z_stats[i, n]
    turned = zt[...].T
    which = (iota((8, 128), 1) % 16 + 4) % 8
    tops = jnp.zeros((8, 128), jnp.float32)
    totals = tops
    for j in range(8):
        tops = jnp.where(which == j, turned[8 * j : 8 * j + 8], tops)
        totals = jnp.where(which == j, turned[PART + 8 * j : PART + 8 * j + 8], totals)
    sizes, tops, totals = tops[:, 16:32], tops[:, 0:16], totals[:, 0:16]
    top = jnp.max(tops, axis=1, keepdims=True)
    weight = jnp.exp(tops - top)
    total = jnp.sum(weight * totals, axis=1, keepdims=True)
    weight = weight * sizes / total
    weight = jnp.concatenate([weight, weight], axis=0)
    context = jnp.zeros((16, 256), jnp.float32)
    wait(z_in.at[1:RING], z_recv.at[1])
    for i in range(RING):
        context += z_in[i].astype(jnp.int32).astype(jnp.float32) * weight[:, i : i + 1]
    out[:, 0:256] = context[0:8]
    out[:, 256:512] = context[8:16]
    out[:, 512:] = jnp.broadcast_to(top + jnp.log(total), (8, 128))

    wait(z_stats.at[1:RING], z_send.at[0])
    wait(z_in.at[1:RING], z_send.at[1])
    wait(qcat.at[1:4, :, 0], q_send)
    wait(qcat.at[1:4, :, 0], f_send)
    wait(stage_l, kv_send)
    wait(stage_r, kr_send)
    wait(r0_acc, r0_send)
    wait(h_st, r1_send.at[0])
    wait(h_acc, r1_send.at[1])


def layout_kernel(rows, ctx_out, log_out):
    for q in range(4):
        ctx_out[q] = rows[2 * q : 2 * q + 2, 0:LAT].astype(jnp.bfloat16)
    cell, spot = iota((8, 128), 0), iota((8, 128), 1)
    for h in range(2):
        line = jnp.where((cell % 2 == h) & (spot == cell // 2), rows[:, LAT:], 0.0)
        log_out[h : h + 1, :] = jnp.sum(line, axis=0, keepdims=True)[:, 0:4]


def per_device(q_latent, q_rope, pool_latent, pool_rope, page_table, lengths, slot_request):
    vmem = pl.BlockSpec(memory_space=pltpu.VMEM)
    anywhere = pl.BlockSpec(memory_space=pl.ANY)
    f32, bf16, i32, i16 = jnp.float32, jnp.bfloat16, jnp.int32, jnp.int16
    dma = pltpu.SemaphoreType.DMA
    rows = pl.pallas_call(
        kernel,
        out_shape=jax.ShapeDtypeStruct((8, LAT + 128), f32),
        in_specs=[anywhere] * 7,
        out_specs=vmem,
        scratch_shapes=[
            pltpu.SMEM((16,), i32),
            pltpu.SMEM((16,), i32),
            pltpu.VMEM((16, MAXP), i32),
            pltpu.VMEM((ROWS, LAT), bf16),
            pltpu.VMEM((4, 64 * ROPE), bf16),
            pltpu.VMEM((PAGES, TOK, LAT), bf16),
            pltpu.VMEM((PAGES, TOK * ROPE), bf16),
            pltpu.VMEM((33 * PAGES, 128), f32),
            pltpu.VMEM((16, MAXP), i32),
            pltpu.VMEM((16, MAXP), i32),
            pltpu.VMEM((32, 128), i32),
            pltpu.SMEM((32, 128), i32),
            pltpu.VMEM((12, CAP, TOK, LAT), bf16),
            pltpu.VMEM((12, CAP, 32, 128), bf16),
            pltpu.VMEM((4, CAP, 4, TOK, LAT), bf16),
            pltpu.VMEM((4, CAP, 4, 32, 128), bf16),
            pltpu.VMEM((4, SPAN, 128), bf16),
            pltpu.VMEM((128, 128), f32),
            pltpu.VMEM((4, 2, 2, PART, LAT + 128), bf16),
            pltpu.VMEM((128, SPAN), f32),
            pltpu.VMEM((128, SPAN), bf16),
            pltpu.VMEM((4, 2, 2, PART, LAT + 128), f32),
            pltpu.VMEM((4, 2, PART, LAT + 128), f32),
            pltpu.VMEM((3, 2, PART, LAT), i16),
            pltpu.VMEM((3, 2, 8, 128), f32),
            pltpu.VMEM((2, 3, PART, LAT), i16),
            pltpu.VMEM((2, 3, 8, 128), f32),
            pltpu.VMEM((2, 8, 16, 256), i16),
            pltpu.VMEM((2, 2, 1, 128), f32),
            pltpu.VMEM((RING, 16, 256), i16),
            pltpu.VMEM((RING, 2, 1, 128), f32),
            pltpu.VMEM((128, 128), f32),
            dma((7,)),
            dma,
            dma,
            dma((4,)),
            dma,
            dma((4,)),
            dma,
            dma((4,)),
            dma,
            dma((4,)),
            dma,
            dma((4, 2)),
            dma((2,)),
            dma((2, 2)),
            dma((2,)),
            dma((2,)),
        ],
        compiler_params=pltpu.CompilerParams(
            collective_id=0, has_side_effects=True, vmem_limit_bytes=60 * 2**20
        ),
        cost_estimate=pl.CostEstimate(flops=2 * 10**9, bytes_accessed=4 * 10**6, transcendentals=10**6),
    )(
        slot_request,
        lengths,
        page_table,
        q_latent.reshape(ROWS, LAT),
        q_rope.reshape(4, 64 * ROPE),
        pool_latent,
        pool_rope,
    )
    ctx, log = pl.pallas_call(
        layout_kernel,
        out_shape=(jax.ShapeDtypeStruct((4, 2, LAT), bf16), jax.ShapeDtypeStruct((2, 4), f32)),
        in_specs=[vmem],
        out_specs=(vmem, vmem),
        compiler_params=pltpu.CompilerParams(vmem_limit_bytes=60 * 2**20),
    )(rows)
    return ctx.reshape(1, 4, 2, LAT), log.T.reshape(1, 4, 2)


def solution(mesh):
    in_specs = (
        P("pool", None, None, None),
        P("pool", None, None),
        P(("pool", "dcp"), None, None),
        P(("pool", "dcp"), None),
        P(),
        P(),
        P(),
    )
    out_specs = (P("pool", None, "dcp", None), P("pool", None, "dcp"))
    return jax.shard_map(
        per_device, mesh=mesh, in_specs=in_specs, out_specs=out_specs, check_vma=False
    )
```
